512 devices in a mesh: row: 32 (over x_lo, z), col: 16 (over y, x_hi, core).
Axes of the slice: x: 4 (x_hi: 2, x_lo: 2; x = x_hi * 2 + x_lo), y: 4, z: 16, core: 2. Of those that a mesh axis runs over, the one named last changes fastest.
Arguments:
- inputs: bfloat16 [512, 20480], P('row', 'col'), may hold values from -6 to 6
- weight: bfloat16 [20480, 20480], P('col', 'row'), may hold values from -0.0390625 to 0.0390625
- out_grad: bfloat16 [512, 20480], P('col', 'row'), may hold values from -6 to 6
Outputs:
- queries: bfloat16 [512, 20480], P('col', 'row')
- input_grad: bfloat16 [512, 20480], P('row', 'col')
- weight_grad: bfloat16 [20480, 20480], P('col', 'row')
The draws below stay inside these ranges and needn't reach their ends.
All inputs are finite; a program needn't handle non-finite values.
Results may differ from the reference program's by a relative error of at most 0.001.
Values may be sent and summed in bfloat16 or wider, within the bound.
No kernel may reach another device: no remote copies, remote signals or barrier semaphores. Data moves between devices by JAX's collectives and lax.ppermute only.
A program may use at most 64 MiB of HBM per device.

```python
import jax
import jax.numpy as jnp

D = 20480
NQ = 20480
TOKENS = 512


def block_scale(own_key, shape, pieces, low, top_value):
    def one(position, blocks):
        heights = jax.random.uniform(jax.random.fold_in(jax.random.fold_in(own_key, 6), position), (blocks,), jnp.float32, low / len(pieces), top_value / len(pieces))
        return jnp.repeat(jnp.exp(heights), shape[position] // blocks).reshape((-1,) + (1,) * (len(shape) - position - 1))

    loudness = one(*pieces[0])
    for cut in pieces[1:]:
        loudness = loudness * one(*cut)
    return loudness


def centred(key, shape, width, bound, split=(), held_as=jnp.bfloat16):
    result = jax.random.normal(key, shape, jnp.float32) * width
    if len(split) > 0:
        result = block_scale(key, shape, split, -0.22, 0.18) * result
    return jnp.clip(result, min=-bound, max=bound).astype(held_as)


def setup_inputs(seed: int = 0) -> dict:
    splits = jax.random.split(jax.random.key(seed), 4)
    inputs = centred(splits[0], (TOKENS, D), 1.0, 6.0, ((0, 32), (1, 16)))
    weight = centred(splits[1], (D, NQ), D ** -0.5, 0.0390625, ((0, 16), (1, 32)))
    out_grad = centred(splits[2], (TOKENS, NQ), 1.0, 6.0, ((0, 16), (1, 32)))
    return {"inputs": inputs, "weight": weight, "out_grad": out_grad}


def reference(inputs, weight, out_grad):
    queries = jnp.dot(inputs, weight, preferred_element_type=jnp.float32).astype(jnp.bfloat16)
    input_grad = jnp.dot(out_grad, weight.T, preferred_element_type=jnp.float32).astype(jnp.bfloat16)
    scale = 1.0 / jnp.sqrt(jnp.float32(TOKENS))
    weight_grad = (jnp.dot(inputs.T, out_grad, preferred_element_type=jnp.float32) * scale).astype(jnp.bfloat16)
    return (queries, input_grad, weight_grad)
```

```python
import jax
import jax.numpy as jnp
from jax import lax
from jax.sharding import Mesh, PartitionSpec as P

ROW = ("xl", "z")
COL = ("y", "xh", "core")
PLANE = ("xl",) + COL
F32 = jnp.float32


def swap_pair(x):
    return lax.ppermute(x, "xl", [(0, 1), (1, 0)])


def gather(x, axes, n):
    return lax.all_to_all(jnp.broadcast_to(x[None], (n,) + x.shape), axes, 0, 0, tiled=True)


def on_device(inputs, weight, out_grad):
    xl = lax.axis_index("xl")
    weight_other = swap_pair(weight)
    grads = gather(out_grad, PLANE, 32).reshape(2, 512, 640)
    grad_own = lax.dynamic_index_in_dim(grads, xl, 0, keepdims=False)
    grad_other = lax.dynamic_index_in_dim(grads, 1 - xl, 0, keepdims=False)
    half = lambda g: lax.dynamic_slice_in_dim(g, xl * 256, 256, 0)
    nt = (((1,), (1,)), ((), ()))
    partial = lax.dot_general(half(grad_own), weight, nt, preferred_element_type=F32)
    partial += lax.dot_general(half(grad_other), weight_other, nt, preferred_element_type=F32)
    parts = lax.all_to_all(partial.reshape(16, 16, 1280), "z", 0, 0, tiled=True)
    input_grad = parts.sum(0).astype(jnp.bfloat16)

    own = gather(inputs, "z", 16).reshape(256, 1280)
    other = swap_pair(own)
    rows = jnp.where(xl == 0, jnp.concatenate([own, other]), jnp.concatenate([other, own]))
    q = jnp.dot(rows, weight, preferred_element_type=F32)
    q = lax.all_to_all(q.reshape(16, 32, 640), COL, 0, 0, tiled=True)
    queries = q.sum(0).astype(jnp.bfloat16)

    scale = 1.0 / jnp.sqrt(F32(512))
    product = lax.dot_general(rows, grad_own, (((0,), (0,)), ((), ())), preferred_element_type=F32)
    weight_grad = (product * scale).astype(jnp.bfloat16)
    return (queries, input_grad, weight_grad)


def solution(mesh):
    fine = Mesh(mesh.devices.reshape(2, 16, 4, 2, 2), ROW + COL)
    placed = (P(ROW, COL), P(COL, ROW), P(COL, ROW))
    return jax.shard_map(
        on_device,
        mesh=fine,
        in_specs=placed,
        out_specs=(P(COL, ROW), P(ROW, COL), P(COL, ROW)),
        check_vma=False,
    )
```

```python
import jax
import jax.numpy as jnp
from jax import lax
from jax.sharding import Mesh, PartitionSpec as P

ROW = ("xl", "z")
COL = ("yh", "yl", "xh", "core")
F32 = jnp.float32
BF16 = jnp.bfloat16
F16 = jnp.float16
NT = (((1,), (1,)), ((), ()))


def swap(x, axis):
    return lax.ppermute(x, axis, [(0, 1), (1, 0)])


def pick(x, i, axis):
    return lax.dynamic_index_in_dim(x, i, axis, keepdims=False)


def ordered(mine, other, i, axis):
    return jnp.where(i == 0, jnp.stack([mine, other], axis), jnp.stack([other, mine], axis))


def encode(rows):
    top = jnp.max(jnp.abs(rows), axis=-1, keepdims=True)
    power = jnp.clip(jnp.ceil(jnp.log2(top)), -100.0, 100.0)
    v = rows * jnp.exp2(-power)
    coded = (v * jnp.abs(v) * 8192.0).astype(F16)
    tail = jnp.broadcast_to(power.astype(F16), rows.shape[:-1] + (128,))
    return jnp.concatenate([coded, tail], axis=-1)


def decode(coded):
    u = coded[..., :-128].astype(F32)
    power = coded[..., -128:-127].astype(F32)
    return jnp.sign(u) * jnp.sqrt(jnp.abs(u) * (1.0 / 8192.0)) * jnp.exp2(power)


def on_device(inputs, weight, out_grad):
    xl, z, yh, yl, xh, core = (lax.axis_index(a) for a in ROW + COL)
    weight_other = swap(weight, "xl")

    spread = jnp.broadcast_to(out_grad[None], (32, 32, 640))
    grads = lax.all_to_all(spread, ("xl",) + COL, 0, 0, tiled=True).reshape(2, 512, 640)

    own = lax.all_gather(inputs, "z", axis=0, tiled=True)
    own, grads = lax.optimization_barrier((own, grads))

    grad_own, grad_other = pick(grads, xl, 0), pick(grads, 1 - xl, 0)
    half = lambda g: lax.dynamic_slice_in_dim(g, xl * 256, 256, 0)
    partial = lax.dot_general(half(grad_own), weight, NT, preferred_element_type=F32)
    partial += lax.dot_general(half(grad_other), weight_other, NT, preferred_element_type=F32)
    parts = lax.all_to_all(encode(partial.reshape(16, 16, 1280)), "z", 0, 0, tiled=True)
    input_grad = decode(parts).sum(0).astype(BF16)

    q = jnp.stack([jnp.dot(own, w, preferred_element_type=F32) for w in (weight, weight_other)])
    q = q.reshape(2, 2, 2, 2, 32, 640)
    for name, i, axis in (("core", core, 3), ("xh", xh, 2), ("yl", yl, 1)):
        q = pick(q, i, axis) + swap(pick(q, 1 - i, axis), name)
    own, q = lax.optimization_barrier((own, q))
    same = xl == yh
    first = lax.ppermute(jnp.where(same, q[1], q[0]), ("xl", "yh"), [(0, 2), (1, 0), (2, 3), (3, 1)])
    second = lax.ppermute(q[1], ("xl", "yh"), [(1, 2), (2, 1)])
    queries = (first + jnp.where(same, q[0], second)).astype(BF16)

    rows = ordered(own, swap(own, "xl"), xl, 0).reshape(512, 1280)
    scale = 1.0 / jnp.sqrt(F32(512))
    product = lax.dot_general(rows, grad_own, (((0,), (0,)), ((), ())), preferred_element_type=F32)
    weight_grad = (product * scale).astype(BF16)
    return (queries, input_grad, weight_grad)


def solution(mesh):
    fine = Mesh(mesh.devices.reshape(2, 16, 2, 2, 2, 2), ROW + COL)
    placed = (P(ROW, COL), P(COL, ROW), P(COL, ROW))
    return jax.shard_map(
        on_device,
        mesh=fine,
        in_specs=placed,
        out_specs=(P(COL, ROW), P(ROW, COL), P(COL, ROW)),
        check_vma=False,
    )
```

```python
import jax
import jax.numpy as jnp
from jax import lax
from jax.experimental import pallas as pl
from jax.experimental.pallas import tpu as pltpu
from jax.sharding import Mesh, PartitionSpec as P

ROW = ("xl", "z")
COL = ("yh", "yl", "xh", "core")
F32 = jnp.float32
BF16 = jnp.bfloat16
NT = (((1,), (1,)), ((), ()))


def swap(x, axis):
    return lax.ppermute(x, axis, [(0, 1), (1, 0)])


def pick(x, i, axis):
    return lax.dynamic_index_in_dim(x, i, axis, keepdims=False)


def ordered(mine, other, i, axis):
    return jnp.where(i == 0, jnp.stack([mine, other], axis), jnp.stack([other, mine], axis))


def encode_kernel(half, g_own, g_other, w_own, w_other, out):
    rows = lax.dot_general(g_own[0], w_own[...], NT, preferred_element_type=F32)
    rows += lax.dot_general(g_other[0], w_other[...], NT, preferred_element_type=F32)
    top = jnp.maximum(jnp.max(jnp.abs(rows), axis=-1, keepdims=True), 1e-30)
    power = jnp.clip(jnp.ceil(jnp.log2(top)), -100.0, 100.0)
    v = rows * jnp.exp2(-power)
    u = v * v
    u = u * u
    u = u * u * 2.0**60
    u = u * u
    out[:, :1280] = jnp.where(v < 0, -u, u).astype(BF16)
    out[:, 1280:] = jnp.broadcast_to(power, (rows.shape[0], 128)).astype(BF16)


def encode(grads, xl, weight, weight_other):
    tile = 128
    n = 256 // tile
    whole = pl.BlockSpec((1280, 640), lambda i, h: (0, 0))
    return pl.pallas_call(
        encode_kernel,
        grid_spec=pltpu.PrefetchScalarGridSpec(
            num_scalar_prefetch=1,
            grid=(n,),
            in_specs=[
                pl.BlockSpec((1, tile, 640), lambda i, h: (h[0], h[0] * n + i, 0)),
                pl.BlockSpec((1, tile, 640), lambda i, h: (1 - h[0], h[0] * n + i, 0)),
                whole,
                whole,
            ],
            out_specs=pl.BlockSpec((tile, 1408), lambda i, h: (i, 0)),
        ),
        out_shape=jax.ShapeDtypeStruct((256, 1408), BF16),
        compiler_params=pltpu.CompilerParams(vmem_limit_bytes=32 << 20),
        cost_estimate=pl.CostEstimate(flops=850_000_000, bytes_accessed=5_000_000, transcendentals=0),
    )(xl.reshape(1).astype(jnp.int32), grads, grads, weight, weight_other)


def decode_kernel(parts, out):
    total = jnp.zeros((16, 1280), F32)
    for i in range(16):
        u = parts[i, :, :1280].astype(F32)
        power = parts[i, :, 1280:].astype(F32)[:, :1]
        size = jnp.abs(u)
        root = jnp.exp2(jnp.log2(jnp.maximum(size, 1e-37)) * (1.0 / 16.0) + (power - 7.5))
        total += jnp.where(size > 1e-37, jnp.where(u < 0, -root, root), 0.0)
    out[...] = total.astype(BF16)


def decode(parts):
    return pl.pallas_call(
        decode_kernel,
        out_shape=jax.ShapeDtypeStruct((16, 1280), BF16),
        compiler_params=pltpu.CompilerParams(vmem_limit_bytes=32 << 20),
    )(parts)


def on_device(inputs, weight, out_grad):
    xl, z, yh, yl, xh, core = (lax.axis_index(a) for a in ROW + COL)
    weight_other = swap(weight, "xl")

    spread = jnp.broadcast_to(out_grad[None], (32, 32, 640))
    grads = lax.all_to_all(spread, ("xl",) + COL, 0, 0, tiled=True).reshape(2, 512, 640)

    own = lax.all_gather(inputs, "z", axis=0, tiled=True)
    own, weight_other = lax.optimization_barrier((own, weight_other))
    own_other = swap(own, "xl")
    by_core = own.reshape(2, 2, 2, 32, 1280)

    def project(i):
        x = pick(by_core, i, 2).reshape(128, 1280)
        return jnp.stack([jnp.dot(x, w, preferred_element_type=F32) for w in (weight, weight_other)])

    sent = project(1 - core)
    sent, grads = lax.optimization_barrier((sent, grads))
    parts = lax.all_to_all(encode(grads, xl, weight, weight_other).reshape(16, 16, 1408), "z", 0, 0, tiled=True)
    input_grad = decode(parts)

    q = (project(core) + swap(sent, "core")).reshape(2, 2, 2, 32, 640)
    own_other, q = lax.optimization_barrier((own_other, q))
    for name, i, axis in (("xh", xh, 2), ("yl", yl, 1)):
        q = pick(q, i, axis) + swap(pick(q, 1 - i, axis), name)
    same = xl == yh
    first = lax.ppermute(jnp.where(same, q[1], q[0]), ("xl", "yh"), [(0, 2), (1, 0), (2, 3), (3, 1)])
    second = lax.ppermute(q[1], ("xl", "yh"), [(1, 2), (2, 1)])
    queries = (first + jnp.where(same, q[0], second)).astype(BF16)

    rows = ordered(own, own_other, xl, 0).reshape(512, 1280)
    scale = 1.0 / jnp.sqrt(F32(512))
    grad_own = pick(grads, xl, 0)
    product = lax.dot_general(rows, grad_own, (((0,), (0,)), ((), ())), preferred_element_type=F32)
    weight_grad = (product * scale).astype(BF16)
    return (queries, input_grad, weight_grad)


def solution(mesh):
    fine = Mesh(mesh.devices.reshape(2, 16, 2, 2, 2, 2), ROW + COL)
    placed = (P(ROW, COL), P(COL, ROW), P(COL, ROW))
    return jax.shard_map(
        on_device,
        mesh=fine,
        in_specs=placed,
        out_specs=(P(COL, ROW), P(ROW, COL), P(COL, ROW)),
        check_vma=False,
    )
```

```python
import jax
import jax.numpy as jnp
from jax import lax
from jax.experimental import pallas as pl
from jax.experimental.pallas import tpu as pltpu
from jax.sharding import Mesh, PartitionSpec as P

ROW = ("xl", "z")
COL = ("yh", "yl", "xh", "core")
F32 = jnp.float32
BF16 = jnp.bfloat16
NT = (((1,), (1,)), ((), ()))


def swap(x, axis):
    return lax.ppermute(x, axis, [(0, 1), (1, 0)])


def pick(x, i, axis):
    return lax.dynamic_index_in_dim(x, i, axis, keepdims=False)


def ordered(mine, other, i, axis):
    return jnp.where(i == 0, jnp.stack([mine, other], axis), jnp.stack([other, mine], axis))


def encode_rows(g_own, g_other, w_own, w_other, out):
    rows = lax.dot_general(g_own[0], w_own[...], NT, preferred_element_type=F32)
    rows += lax.dot_general(g_other[0], w_other[...], NT, preferred_element_type=F32)
    top = jnp.maximum(jnp.max(jnp.abs(rows), axis=-1, keepdims=True), 1e-30)
    power = jnp.clip(jnp.ceil(jnp.log2(top)), -100.0, 100.0)
    v = rows * jnp.exp2(-power)
    u = v * v
    u = u * u
    u = u * u * 2.0**60
    u = u * u
    out[:, 0, :, :1280] = jnp.where(v < 0, -u, u).astype(BF16).reshape(4, 32, 1280)
    out[:, 0, :, 1280:] = jnp.broadcast_to(power, (128, 128)).astype(BF16).reshape(4, 32, 128)


def encode_kernel(place, g_own, g_other, s_own, s_other, w_own, w_other, out):
    @pl.when(pl.program_id(0) == 0)
    def _():
        encode_rows(g_own, g_other, w_own, w_other, out)

    @pl.when(pl.program_id(0) == 1)
    def _():
        encode_rows(s_own, s_other, w_own, w_other, out)


def encode(mine, swapped, xl, core, weight, weight_other):
    own = pl.BlockSpec((1, 128, 640), lambda i, at: (at[0], at[0], 0))
    other = pl.BlockSpec((1, 128, 640), lambda i, at: (1 - at[0], at[0], 0))
    whole = pl.BlockSpec((1280, 640), lambda i, at: (0, 0))
    return pl.pallas_call(
        encode_kernel,
        grid_spec=pltpu.PrefetchScalarGridSpec(
            num_scalar_prefetch=1,
            grid=(2,),
            in_specs=[own, other, own, other, whole, whole],
            out_specs=pl.BlockSpec((4, 1, 32, 1408), lambda i, at: (0, at[1] + i - 2 * at[1] * i, 0, 0)),
        ),
        out_shape=jax.ShapeDtypeStruct((4, 2, 32, 1408), BF16),
        compiler_params=pltpu.CompilerParams(vmem_limit_bytes=32 << 20),
        cost_estimate=pl.CostEstimate(flops=850_000_000, bytes_accessed=5_000_000, transcendentals=0),
    )(jnp.stack([xl, core]).astype(jnp.int32), mine, mine, swapped, swapped, weight, weight_other)


def decode_kernel(parts, out):
    total = jnp.zeros((16, 1280), F32)
    for i in range(16):
        u = parts[i, :, :1280].astype(F32)
        power = parts[i, :, 1280:].astype(F32)[:, :1]
        size = jnp.abs(u)
        root = jnp.exp2(jnp.log2(jnp.maximum(size, 1e-37)) * (1.0 / 16.0) + (power - 7.5))
        total += jnp.where(size > 1e-37, jnp.where(u < 0, -root, root), 0.0)
    out[...] = total.astype(BF16)


def decode(parts):
    return pl.pallas_call(
        decode_kernel,
        out_shape=jax.ShapeDtypeStruct((16, 1280), BF16),
        compiler_params=pltpu.CompilerParams(vmem_limit_bytes=32 << 20),
    )(parts)


def on_device(inputs, weight, out_grad):
    xl, z, yh, yl, xh, core = (lax.axis_index(a) for a in ROW + COL)
    weight_other = swap(weight, "xl")

    spread = jnp.broadcast_to(out_grad[None], (16, 32, 640))
    grads = lax.all_to_all(spread, ("xl",) + COL[:3], 0, 0, tiled=True).reshape(2, 256, 640)

    own = lax.all_gather(inputs, "z", axis=0, tiled=True)
    own, weight_other = lax.optimization_barrier((own, weight_other))
    def project(rows, i):
        x = pick(rows.reshape(2, 2, 2, 32, 1280), i, 2).reshape(128, 1280)
        return jnp.stack([jnp.dot(x, w, preferred_element_type=F32) for w in (weight, weight_other)])

    sent = project(own, 1 - core)
    sent, grads = lax.optimization_barrier((sent, grads))
    swapped = swap(grads, "core")
    coded = encode(grads, swapped, xl, core, weight, weight_other)
    own_other = swap(own, "xl")
    own, coded = lax.optimization_barrier((own, coded))
    parts = lax.all_to_all(coded.reshape(16, 16, 1408), "z", 0, 0, tiled=True)
    input_grad = decode(parts)

    q = (project(own, core) + swap(sent, "core")).reshape(2, 2, 2, 32, 640)
    own_other, q = lax.optimization_barrier((own_other, q))
    for name, i, axis in (("xh", xh, 2), ("yl", yl, 1)):
        q = pick(q, i, axis) + swap(pick(q, 1 - i, axis), name)
    same = xl == yh
    first = lax.ppermute(jnp.where(same, q[1], q[0]), ("xl", "yh"), [(0, 2), (1, 0), (2, 3), (3, 1)])
    second = lax.ppermute(q[1], ("xl", "yh"), [(1, 2), (2, 1)])
    queries = (first + jnp.where(same, q[0], second)).astype(BF16)

    rows = ordered(own, own_other, xl, 0).reshape(512, 1280)
    scale = 1.0 / jnp.sqrt(F32(512))
    grad_own = [pick(g, xl, 0).reshape(8, 32, 640) for g in (grads, swapped)]
    grad_own = ordered(*grad_own, core, 1).reshape(512, 640)
    product = lax.dot_general(rows, grad_own, (((0,), (0,)), ((), ())), preferred_element_type=F32)
    weight_grad = (product * scale).astype(BF16)
    return (queries, input_grad, weight_grad)


def solution(mesh):
    fine = Mesh(mesh.devices.reshape(2, 16, 2, 2, 2, 2), ROW + COL)
    placed = (P(ROW, COL), P(COL, ROW), P(COL, ROW))
    return jax.shard_map(
        on_device,
        mesh=fine,
        in_specs=placed,
        out_specs=(P(COL, ROW), P(ROW, COL), P(COL, ROW)),
        check_vma=False,
    )
```

```python
import jax
import jax.numpy as jnp
from jax import lax
from jax.experimental import pallas as pl
from jax.experimental.pallas import tpu as pltpu
from jax.sharding import Mesh, PartitionSpec as P

ROW = ("xl", "z")
COL = ("yh", "yl", "xh", "core")
F32 = jnp.float32
BF16 = jnp.bfloat16
NT = (((1,), (1,)), ((), ()))


def swap(x, axis):
    return lax.ppermute(x, axis, [(0, 1), (1, 0)])


def pick(x, i, axis):
    return lax.dynamic_index_in_dim(x, i, axis, keepdims=False)


def ordered(mine, other, i, axis):
    return jnp.where(i == 0, jnp.stack([mine, other], axis), jnp.stack([other, mine], axis))


def encode_kernel(place, g_own, g_other, s_own, s_other, w_own, w_other, out):
    own = jnp.concatenate([g_own[0], s_own[0]], axis=0)
    other = jnp.concatenate([g_other[0], s_other[0]], axis=0)
    rows = lax.dot_general(own, w_own[...], NT, preferred_element_type=F32)
    rows += lax.dot_general(other, w_other[...], NT, preferred_element_type=F32)
    top = jnp.maximum(jnp.max(jnp.abs(rows), axis=-1, keepdims=True), 1e-30)
    power = jnp.clip(jnp.ceil(jnp.log2(top)), -100.0, 100.0)
    v = rows * jnp.exp2(-power)
    u = v * v
    u = u * u
    u = u * u * 2.0**60
    u = u * u
    coded = jnp.where(v < 0, -u, u).astype(BF16)
    tail = jnp.broadcast_to(power, (256, 128)).astype(BF16)
    for i, core in enumerate((place[1], 1 - place[1])):
        at = pl.ds(core, 1)
        out[:, at, :, :1280] = coded[i * 128 : i * 128 + 128].reshape(4, 1, 32, 1280)
        out[:, at, :, 1280:] = tail[i * 128 : i * 128 + 128].reshape(4, 1, 32, 128)


def encode(mine, swapped, xl, core, weight, weight_other):
    own = pl.BlockSpec((1, 128, 640), lambda i, at: (at[0], at[0], 0))
    other = pl.BlockSpec((1, 128, 640), lambda i, at: (1 - at[0], at[0], 0))
    whole = pl.BlockSpec((1280, 640), lambda i, at: (0, 0))
    return pl.pallas_call(
        encode_kernel,
        grid_spec=pltpu.PrefetchScalarGridSpec(
            num_scalar_prefetch=1,
            grid=(1,),
            in_specs=[own, other, own, other, whole, whole],
            out_specs=pl.BlockSpec((4, 2, 32, 1408), lambda i, at: (0, 0, 0, 0)),
        ),
        out_shape=jax.ShapeDtypeStruct((4, 2, 32, 1408), BF16),
        compiler_params=pltpu.CompilerParams(vmem_limit_bytes=32 << 20),
        cost_estimate=pl.CostEstimate(flops=850_000_000, bytes_accessed=5_000_000, transcendentals=0),
    )(jnp.stack([xl, core]).astype(jnp.int32), mine, mine, swapped, swapped, weight, weight_other)


def decode_kernel(parts, powers, out):
    total = jnp.zeros(out.shape, F32)
    for i in range(16):
        u = parts[i].astype(F32)
        power = powers[i].astype(F32)[:, :1]
        size = jnp.abs(u)
        root = jnp.exp2(jnp.log2(jnp.maximum(size, 1e-37)) * (1.0 / 16.0) + (power - 7.5))
        total += jnp.where(size > 1e-37, jnp.where(u < 0, -root, root), 0.0)
    out[...] = total.astype(BF16)


def decode(parts):
    return pl.pallas_call(
        decode_kernel,
        grid=(2,),
        in_specs=[
            pl.BlockSpec((16, 16, 640), lambda i: (0, 0, i)),
            pl.BlockSpec((16, 16, 128), lambda i: (0, 0, 10)),
        ],
        out_specs=pl.BlockSpec((16, 640), lambda i: (0, i)),
        out_shape=jax.ShapeDtypeStruct((16, 1280), BF16),
        compiler_params=pltpu.CompilerParams(vmem_limit_bytes=32 << 20),
    )(parts, parts)


def on_device(inputs, weight, out_grad):
    xl, z, yh, yl, xh, core = (lax.axis_index(a) for a in ROW + COL)
    weight_other = swap(weight, "xl")

    spread = jnp.broadcast_to(out_grad[None], (16, 32, 640))
    grads = lax.all_to_all(spread, ("xl",) + COL[:3], 0, 0, tiled=True).reshape(2, 256, 640)

    own = lax.all_gather(inputs, "z", axis=0, tiled=True)
    own, weight_other = lax.optimization_barrier((own, weight_other))
    def project(rows, i):
        x = pick(rows.reshape(2, 2, 2, 32, 1280), i, 2).reshape(128, 1280)
        return jnp.stack([jnp.dot(x, w, preferred_element_type=F32) for w in (weight, weight_other)])

    sent = project(own, 1 - core)
    sent, grads = lax.optimization_barrier((sent, grads))
    swapped = swap(grads, "core")
    coded = encode(grads, swapped, xl, core, weight, weight_other)
    own_other = swap(own, "xl")
    own, grads, swapped, coded = lax.optimization_barrier((own, grads, swapped, coded))
    parts = lax.all_to_all(coded.reshape(16, 16, 1408), "z", 0, 0, tiled=True)
    input_grad = decode(parts)

    q = (project(own, core) + swap(sent, "core")).reshape(2, 2, 2, 32, 640)
    own_other, q = lax.optimization_barrier((own_other, q))
    piece = lambda j, k: pick(pick(q, k, 2), j, 1)
    across = lax.ppermute(piece(1 - yl, 1 - xh), ("yl", "xh"), [(0, 3), (1, 2), (2, 1), (3, 0)])
    q = piece(yl, xh) + swap(piece(yl, 1 - xh), "xh") + swap(piece(1 - yl, xh), "yl") + across
    same = xl == yh
    first = lax.ppermute(jnp.where(same, q[1], q[0]), ("xl", "yh"), [(0, 2), (1, 0), (2, 3), (3, 1)])
    second = lax.ppermute(q[1], ("xl", "yh"), [(1, 2), (2, 1)])
    queries = (first + jnp.where(same, q[0], second)).astype(BF16)

    rows = ordered(own, own_other, xl, 0).reshape(512, 1280)
    scale = 1.0 / jnp.sqrt(F32(512))
    grad_own = [pick(g, xl, 0).reshape(8, 32, 640) for g in (grads, swapped)]
    grad_own = ordered(*grad_own, core, 1).reshape(512, 640)
    product = lax.dot_general(rows, grad_own, (((0,), (0,)), ((), ())), preferred_element_type=F32)
    weight_grad = (product * scale).astype(BF16)
    return (queries, input_grad, weight_grad)


def solution(mesh):
    fine = Mesh(mesh.devices.reshape(2, 16, 2, 2, 2, 2), ROW + COL)
    placed = (P(ROW, COL), P(COL, ROW), P(COL, ROW))
    return jax.shard_map(
        on_device,
        mesh=fine,
        in_specs=placed,
        out_specs=(P(COL, ROW), P(ROW, COL), P(COL, ROW)),
        check_vma=False,
    )
```

```python
import jax
import jax.numpy as jnp
from jax import lax
from jax.experimental import pallas as pl
from jax.experimental.pallas import tpu as pltpu
from jax.sharding import Mesh, PartitionSpec as P

ROW = ("xl", "z")
COL = ("yh", "yl", "xh", "core")
F32 = jnp.float32
BF16 = jnp.bfloat16
NT = (((1,), (1,)), ((), ()))


def swap(x, axis):
    return lax.ppermute(x, axis, [(0, 1), (1, 0)])


def pick(x, i, axis):
    return lax.dynamic_index_in_dim(x, i, axis, keepdims=False)


def ordered(mine, other, i, axis):
    return jnp.where(i == 0, jnp.stack([mine, other], axis), jnp.stack([other, mine], axis))


def encode_kernel(place, g_own, g_other, s_own, s_other, w_own, w_other, out):
    own = jnp.concatenate([g_own[0], s_own[0]], axis=0)
    other = jnp.concatenate([g_other[0], s_other[0]], axis=0)
    rows = lax.dot_general(own, w_own[...], NT, preferred_element_type=F32)
    rows += lax.dot_general(other, w_other[...], NT, preferred_element_type=F32)
    top = jnp.maximum(jnp.max(jnp.abs(rows), axis=-1, keepdims=True), 1e-30)
    power = jnp.clip(jnp.ceil(jnp.log2(top)), -100.0, 100.0)
    v = rows * jnp.exp2(-power)
    u = v * v
    u = u * u
    u = u * u * 2.0**60
    u = u * u
    coded = jnp.where(v < 0, -u, u).astype(BF16)
    tail = jnp.broadcast_to(power, (256, 128)).astype(BF16)
    for i, core in enumerate((place[1], 1 - place[1])):
        at = pl.ds(core, 1)
        out[:, at, :, :1280] = coded[i * 128 : i * 128 + 128].reshape(4, 1, 32, 1280)
        out[:, at, :, 1280:] = tail[i * 128 : i * 128 + 128].reshape(4, 1, 32, 128)


def encode(mine, swapped, xl, core, weight, weight_other):
    own = pl.BlockSpec((1, 128, 640), lambda i, at: (at[0], at[0], 0))
    other = pl.BlockSpec((1, 128, 640), lambda i, at: (1 - at[0], at[0], 0))
    whole = pl.BlockSpec((1280, 640), lambda i, at: (0, 0))
    return pl.pallas_call(
        encode_kernel,
        grid_spec=pltpu.PrefetchScalarGridSpec(
            num_scalar_prefetch=1,
            grid=(1,),
            in_specs=[own, other, own, other, whole, whole],
            out_specs=pl.BlockSpec((4, 2, 32, 1408), lambda i, at: (0, 0, 0, 0)),
        ),
        out_shape=jax.ShapeDtypeStruct((4, 2, 32, 1408), BF16),
        compiler_params=pltpu.CompilerParams(vmem_limit_bytes=32 << 20),
        cost_estimate=pl.CostEstimate(flops=850_000_000, bytes_accessed=5_000_000, transcendentals=0),
    )(jnp.stack([xl, core]).astype(jnp.int32), mine, mine, swapped, swapped, weight, weight_other)


def decode_kernel(parts, powers, out):
    total = jnp.zeros(out.shape, F32)
    for i in range(16):
        u = parts[i].astype(F32)
        power = powers[i].astype(F32)[:, :1]
        size = jnp.abs(u)
        root = jnp.exp2(jnp.log2(jnp.maximum(size, 1e-37)) * (1.0 / 16.0) + (power - 7.5))
        total += jnp.where(size > 1e-37, jnp.where(u < 0, -root, root), 0.0)
    out[...] = total.astype(BF16)


def decode(parts):
    return pl.pallas_call(
        decode_kernel,
        grid=(2,),
        in_specs=[
            pl.BlockSpec((16, 16, 640), lambda i: (0, 0, i)),
            pl.BlockSpec((16, 16, 128), lambda i: (0, 0, 10)),
        ],
        out_specs=pl.BlockSpec((16, 640), lambda i: (0, i)),
        out_shape=jax.ShapeDtypeStruct((16, 1280), BF16),
        compiler_params=pltpu.CompilerParams(vmem_limit_bytes=32 << 20),
    )(parts, parts)


def on_device(inputs, weight, out_grad):
    xl, z, yh, yl, xh, core = (lax.axis_index(a) for a in ROW + COL)
    weight_other = swap(weight, "xl")

    spread = jnp.broadcast_to(out_grad[None], (16, 32, 640))
    grads = lax.all_to_all(spread, ("xl",) + COL[:3], 0, 0, tiled=True).reshape(2, 256, 640)

    own = lax.all_gather(inputs, "z", axis=0, tiled=True)
    own, weight_other = lax.optimization_barrier((own, weight_other))
    def project(rows, i):
        x = pick(rows.reshape(2, 2, 2, 32, 1280), i, 2).reshape(128, 1280)
        return jnp.stack([jnp.dot(x, w, preferred_element_type=F32) for w in (weight, weight_other)])

    sent = project(own, 1 - core)
    sent, grads = lax.optimization_barrier((sent, grads))
    swapped = swap(grads, "core")
    coded = encode(grads, swapped, xl, core, weight, weight_other)
    own_other = swap(own, "xl")
    own, grads, swapped, sent, coded = lax.optimization_barrier((own, grads, swapped, sent, coded))
    parts = lax.all_to_all(coded.reshape(16, 16, 1408), "z", 0, 0, tiled=True)
    input_grad = decode(parts)

    q = (project(own, core) + swap(sent, "core")).reshape(2, 2, 2, 32, 640)
    own_other, q = lax.optimization_barrier((own_other, q))
    piece = lambda j, k: pick(pick(q, k, 2), j, 1)
    across = lax.ppermute(piece(1 - yl, 1 - xh), ("yl", "xh"), [(0, 3), (1, 2), (2, 1), (3, 0)])
    q = piece(yl, xh) + swap(piece(yl, 1 - xh), "xh") + swap(piece(1 - yl, xh), "yl") + across
    same = xl == yh
    first = lax.ppermute(jnp.where(same, q[1], q[0]), ("xl", "yh"), [(0, 2), (1, 0), (2, 3), (3, 1)])
    second = lax.ppermute(q[1], ("xl", "yh"), [(1, 2), (2, 1)])
    queries = (first + jnp.where(same, q[0], second)).astype(BF16)

    rows = ordered(own, own_other, xl, 0).reshape(512, 1280)
    scale = 1.0 / jnp.sqrt(F32(512))
    grad_own = [pick(g, xl, 0).reshape(8, 32, 640) for g in (grads, swapped)]
    grad_own = ordered(*grad_own, core, 1).reshape(512, 640)
    product = lax.dot_general(rows, grad_own, (((0,), (0,)), ((), ())), preferred_element_type=F32)
    weight_grad = (product * scale).astype(BF16)
    return (queries, input_grad, weight_grad)


def solution(mesh):
    fine = Mesh(mesh.devices.reshape(2, 16, 2, 2, 2, 2), ROW + COL)
    placed = (P(ROW, COL), P(COL, ROW), P(COL, ROW))
    return jax.shard_map(
        on_device,
        mesh=fine,
        in_specs=placed,
        out_specs=(P(COL, ROW), P(ROW, COL), P(COL, ROW)),
        check_vma=False,
    )
```
